32 devices in a mesh: roll: 16 (over z, y, core), seq: 2 (over x).
Axes of the slice: x: 2, y: 2, z: 4, core: 2. Of those that a mesh axis runs over, the one named last changes fastest.
Arguments:
- queries: bfloat16 [8192, 3072], P(('roll', 'seq')), parts along dimension 0, may hold values from -7.5 to 7.5
- keys_in: bfloat16 [8192, 3072], P(('roll', 'seq')), parts along dimension 0, may hold values from -7.5 to 7.5
- values_in: bfloat16 [8192, 3072], P(('roll', 'seq')), parts along dimension 0, may hold values from -6 to 6
- latent_proj: bfloat16 [3072, 64], replicated, may hold values from -3 to 3
- conv_weight: bfloat16 [432, 512], replicated, may hold values from -0.3125 to 0.3125
- conv_bias: float32 [512], replicated, may hold values from -3 to 3
- pool_weight: float32 [2, 2, 8, 64], P('seq'), may hold values from -5 to 5
- tile_block: int32 [128], P('roll'), parts along dimension 0, may hold values from 0 to 7, each once
- owner_slot: int32 [64], P('roll'), parts along dimension 0, may hold values from 0 to 3, each once
Outputs:
- decoded: bfloat16 [32, 2, 8, 64, 512], P(('roll', 'seq')), parts along dimension 0
- policy_features: float32 [64, 512], P(('roll', 'seq')), parts along dimension 0
The draws below stay inside these ranges and needn't reach their ends.
There are 16 independent parts, one for each index of `roll`. The reference program is written for one: setup_inputs(seed, part) draws one part's arguments, and reference() takes and returns one part's arrays. A program takes and returns all parts, laid end to end along the dimension named above; an argument that names none is the same for every part. Nothing has to cross between parts.
Inputs may be any that keep to these rules, and one draw needn't show every extreme that they name: `tile_block`: each piece index once. `owner_slot`: each row once.
All inputs are finite; a program needn't handle non-finite values.
Results may differ from the reference program's by a relative error of at most 0.013.
Values may be sent and summed in bfloat16 or wider, within the bound.
A program may use at most 64 MiB of HBM per device.

```python
import math
import jax
import jax.numpy as jnp
from jax import lax

H = 24
HD = 128
LC = 16
CO = 512
S_DEV = 256
RT = 4
WT = 32
TR = 2
FT = 2
RL = 8
COLS = 64
TILES = 2
PIECES = 8
TF = 1
SEQ = 512
FRAMES = 2
ROWS = 16
NB = 4
VB = 512
KC = 432


def draw_queries(key, part):
    base = jnp.clip(jax.random.normal(jax.random.fold_in(key, 11), (SEQ, H * HD), jnp.float32), -4.0, 4.0)
    return base.astype(jnp.bfloat16)


def draw_keys_in(key, part):
    base = jnp.clip(jax.random.normal(jax.random.fold_in(key, 21), (SEQ, H * HD), jnp.float32), -4.0, 4.0)
    return base.astype(jnp.bfloat16)


def levels(rng, extent, cuts, least, high):
    level, own = 1.0, jax.random.fold_in(rng, 6)
    for axis_at, blocks in cuts:
        steps = jnp.exp(jax.random.uniform(jax.random.fold_in(own, axis_at), (blocks,), jnp.float32, least / len(cuts), high / len(cuts)))
        level = level * jnp.repeat(steps, extent[axis_at] // blocks).reshape([-1 if axis == axis_at else 1 for axis in range(len(extent))])
    return level


def normal_values(own_key, dims, width, reach, split=(), kind=jnp.bfloat16):
    level = levels(own_key, dims, split, -0.22, 0.18) if split else 1.0
    values = jax.random.normal(own_key, dims, jnp.float32) * width * level
    return jnp.minimum(jnp.maximum(values, -reach), reach).astype(kind)


def setup_inputs(seed: int = 0, part: int = 0) -> dict:
    splits = jax.random.split(jax.random.key(seed), 10)
    own_keys = jax.random.split(jax.random.fold_in(splits[9], part), 10)
    return {
        "queries": draw_queries(jax.random.fold_in(jax.random.fold_in(splits[9], part), 71), part),
        "keys_in": draw_keys_in(jax.random.fold_in(jax.random.fold_in(splits[9], part), 71), part),
        "values_in": normal_values(own_keys[2], (SEQ, H * HD), 1.0, 6.0, ((0, 2),)),
        "latent_proj": normal_values(splits[3], (H * HD, 4 * LC), 0.5, 3.0),
        "conv_weight": normal_values(splits[4], (KC, CO), KC ** -0.5, 0.3125),
        "conv_bias": normal_values(splits[5], (CO,), 0.5, 3.0, (), jnp.float32),
        "pool_weight": normal_values(splits[6], (TILES, FT, RL, COLS), 1.0, 5.0, ((0, 2),), jnp.float32),
        "tile_block": jax.random.permutation(own_keys[7], PIECES).astype(jnp.int32),
        "owner_slot": jax.random.permutation(own_keys[8], NB).astype(jnp.int32),
    }


def head_attention(inputs):
    query_head, key_head, value_head = inputs
    scores = jnp.dot(query_head, key_head.T, preferred_element_type=jnp.float32) * (1.0 / math.sqrt(HD))
    expo = jnp.exp(scores - lax.optimization_barrier(jnp.max(scores, axis=-1, keepdims=True)))
    totals = lax.optimization_barrier(jnp.sum(expo, axis=-1, keepdims=True))
    mixed = jnp.dot(expo.astype(jnp.bfloat16), value_head, preferred_element_type=jnp.float32)
    return (mixed / totals).astype(jnp.bfloat16)

def window_columns(volume):
    frame_count = volume.shape[0] - 2
    row_count = volume.shape[1] - 2
    col_count = volume.shape[2] - 2
    pieces = [volume[a:a + frame_count, b:b + row_count, c:c + col_count] for a in range(3) for b in range(3) for c in range(3)]
    return jnp.concatenate(pieces, axis=-1).reshape(frame_count * row_count * col_count, 27 * volume.shape[3])

def split_heads(matrix):
    return matrix.reshape(SEQ, H, HD).transpose(1, 0, 2)

def reference(queries, keys_in, values_in, latent_proj, conv_weight, conv_bias, pool_weight, tile_block, owner_slot):
    heads_out = lax.map(head_attention, (split_heads(queries), split_heads(keys_in), split_heads(values_in)))
    attn_out = heads_out.transpose(1, 0, 2).reshape(SEQ, H * HD)
    latent_tokens = jnp.dot(attn_out, latent_proj, preferred_element_type=jnp.float32).astype(jnp.bfloat16)
    blocks = latent_tokens.reshape(PIECES, S_DEV // 4, 4 * LC)[tile_block]
    blocks = blocks.reshape(TF, TR, FT, RT, WT, 2, 2, LC).transpose(0, 2, 1, 3, 5, 4, 6, 7)
    video = blocks.reshape(FRAMES, ROWS, COLS, LC)
    volume = jnp.pad(video, ((2, 0), (1, 1), (1, 1), (0, 0)))
    pre_act = jnp.dot(window_columns(volume), conv_weight, preferred_element_type=jnp.float32) + conv_bias
    pre_tiles = pre_act.reshape(TF, FT, TR, RL, COLS, CO).transpose(0, 2, 1, 3, 4, 5).reshape(TILES, FT, RL, COLS, CO)
    decoded = pre_tiles.astype(jnp.bfloat16)
    weighted = jax.nn.silu(pre_tiles) * pool_weight[..., None]
    pooled = lax.optimization_barrier(jnp.sum(weighted, axis=(0, 1, 2))).reshape(NB, COLS // NB, CO).sum(axis=1) / math.sqrt(VB)
    policy = jnp.zeros((NB, CO), jnp.float32).at[owner_slot].set(pooled)
    return (decoded, policy)
```

```python
import math

import jax
import jax.numpy as jnp
from jax import lax
from jax.experimental import pallas as pl
from jax.experimental.pallas import tpu as pltpu
from jax.sharding import PartitionSpec as P

H = 24
HD = 128
LC = 16
CO = 512
S_DEV = 256
RT = 4
WT = 32
TR = 2
BPD = 2
FT = 2
RL = 8
COLS = 64


def shifted(array, axis, by):
    length = lax.axis_size(axis)
    pairs = [(i, i + by) for i in range(length) if 0 <= i + by < length]
    return lax.ppermute(array, axis, pairs)


def swapped(array, axis, bit):
    return lax.ppermute(array, axis, [(i, i ^ 1 << bit) for i in range(lax.axis_size(axis))])


def heads_attention(query_all, key_all, value_all):
    length = query_all.shape[0]
    block_rows = min(512, length)
    score_scale = 1.0 / math.sqrt(query_all.shape[2])
    query_blocks = query_all.reshape(
        length // block_rows, block_rows, query_all.shape[1], query_all.shape[2]
    )

    def one_block(query_part):
        scores = (
            jnp.einsum("qhd,khd->hqk", query_part, key_all, preferred_element_type=jnp.float32)
            * score_scale
        )
        expo = jnp.exp(scores - jnp.max(scores, axis=-1, keepdims=True))
        totals = jnp.sum(expo, axis=-1, keepdims=True)
        mixed = jnp.einsum(
            "hqk,khd->qhd", expo.astype(jnp.bfloat16), value_all, preferred_element_type=jnp.float32
        )
        return (mixed / jnp.transpose(totals, (1, 0, 2))).astype(jnp.bfloat16)

    return lax.map(one_block, query_blocks).reshape(length, query_all.shape[1], query_all.shape[2])


def window_columns(volume):
    frame_count = volume.shape[0] - 2
    row_count = volume.shape[1] - 2
    col_count = volume.shape[2] - 2
    pieces = [
        volume[a : a + frame_count, b : b + row_count, c : c + col_count]
        for a in range(3)
        for b in range(3)
        for c in range(3)
    ]
    return jnp.concatenate(pieces, axis=-1).reshape(
        frame_count * row_count * col_count, 27 * volume.shape[3]
    )


def picked(blocks, order):
    count = blocks.shape[0]
    choose = (order[:, None] == jnp.arange(count, dtype=jnp.int32)[None, :]).astype(jnp.bfloat16)
    flat = jnp.dot(choose, blocks.reshape(count, -1), preferred_element_type=jnp.float32)
    return flat.astype(jnp.bfloat16).reshape(blocks.shape)


def local_any(
    queries,
    keys_in,
    values_in,
    latent_proj,
    conv_weight,
    conv_bias,
    pool_weight,
    tile_block,
    owner_slot,
):
    group_count = lax.axis_size("seq")
    my_index = lax.axis_index("seq")
    seq_len = S_DEV * group_count
    heads_dev = H // group_count
    quarter = S_DEV // 4

    def to_groups(matrix):
        return matrix.reshape(S_DEV, group_count, heads_dev, HD)

    query_all = lax.all_to_all(to_groups(queries), "seq", split_axis=1, concat_axis=0, tiled=True)
    key_all = lax.all_to_all(to_groups(keys_in), "seq", split_axis=1, concat_axis=0, tiled=True)
    value_all = lax.all_to_all(to_groups(values_in), "seq", split_axis=1, concat_axis=0, tiled=True)
    mixed = heads_attention(query_all[:, 0], key_all[:, 0], value_all[:, 0])[:, None]
    flat_heads = mixed.reshape(seq_len, heads_dev * HD)
    ordered = picked(flat_heads.reshape(4 * group_count, quarter, heads_dev * HD), tile_block)
    ordered = ordered.reshape(seq_len, 1, heads_dev, HD)
    returned = lax.all_to_all(ordered, "seq", split_axis=0, concat_axis=1, tiled=True)
    tile_heads = returned.reshape(S_DEV, H * HD)
    latent = jnp.dot(tile_heads, latent_proj, preferred_element_type=jnp.float32).astype(
        jnp.bfloat16
    )
    tile_latent = (
        latent.reshape(FT, RT, WT, 2, 2, LC).transpose(0, 1, 3, 2, 4, 5).reshape(FT, RL, COLS * LC)
    )
    earlier = shifted(tile_latent, "seq", TR)
    extended = jnp.concatenate([earlier, tile_latent], axis=0)
    band_row = my_index % TR
    upper_band = band_row == 0
    outgoing = jnp.where(upper_band, extended[:, RL - 1 :], extended[:, :1])
    incoming = swapped(outgoing, "seq", 0)
    above = jnp.where(upper_band, jnp.zeros_like(incoming), incoming)
    below = jnp.where(upper_band, incoming, jnp.zeros_like(incoming))
    volume = jnp.concatenate([above, extended, below], axis=1).reshape(FT + 2, RL + 2, COLS, LC)
    volume = jnp.pad(volume, ((0, 0), (0, 0), (1, 1), (0, 0)))
    pre_act = (
        jnp.dot(window_columns(volume), conv_weight, preferred_element_type=jnp.float32) + conv_bias
    )
    decoded = pre_act.astype(jnp.bfloat16).reshape(1, FT, RL, COLS, CO)
    block_count = BPD * group_count
    band_voxels = group_count // TR * FT * TR * RL * (COLS // block_count)
    weighted = jax.nn.silu(pre_act).reshape(FT, RL, COLS, CO) * pool_weight[0][..., None]
    pooled_term = jnp.sum(weighted, axis=(0, 1)).reshape(block_count, COLS // block_count, CO).sum(
        axis=1
    ) / math.sqrt(band_voxels)
    total_pooled = lax.psum(pooled_term.astype(jnp.bfloat16), "seq").astype(jnp.float32)
    wanted_rows = my_index * BPD + jnp.arange(BPD, dtype=jnp.int32)
    chooser = (owner_slot[None, :] == wanted_rows[:, None]).astype(jnp.float32)
    policy = jnp.dot(
        chooser, total_pooled, precision=lax.Precision.HIGHEST, preferred_element_type=jnp.float32
    )
    return (decoded, policy)


SCALE2 = math.log2(math.e) / math.sqrt(HD)
HALF = S_DEV // 2
COLG = 3
GH = H // COLG
GW = GH * HD
NT = (((1,), (1,)), ((), ()))


def attend_kernel(
    q_hbm,
    k_hbm,
    v_hbm,
    w_hbm,
    lat_out,
    q,
    k,
    v,
    w,
    q_in,
    v_t,
    w_t,
    own,
    stat_own,
    stat_in,
    ret,
    ret_in,
    lat_own,
    lat_in,
    load_sem,
    q_send,
    q_recv,
    small_send,
    small_recv,
):
    me = lax.axis_index("seq")
    other = 1 - me
    loads = [
        pltpu.make_async_copy(src, dst, load_sem.at[i])
        for i, (src, dst) in enumerate(((q_hbm, q), (k_hbm, k), (v_hbm, v), (w_hbm, w)))
    ]
    for load in loads:
        load.start()

    barrier = pltpu.get_barrier_semaphore()
    pl.semaphore_signal(barrier, inc=1, device_id={"seq": other})
    pl.semaphore_wait(barrier, 1)

    def query_copy(half, group):
        rows = pl.ds(half * HALF, HALF)
        start = group * GW
        if not isinstance(group, int):
            start = pl.multiple_of(start, GW)
        part = (rows, pl.ds(start, GW))
        return pltpu.make_async_remote_copy(
            src_ref=q_hbm.at[part],
            dst_ref=q_in.at[part],
            send_sem=q_send.at[half * COLG + group],
            recv_sem=q_recv.at[half * COLG + group],
            device_id={"seq": other},
        )

    def small_copy(src, dst, slot):
        return pltpu.make_async_remote_copy(
            src_ref=src,
            dst_ref=dst,
            send_sem=small_send.at[slot],
            recv_sem=small_recv.at[slot],
            device_id={"seq": other},
        )

    for group in range(COLG):
        query_copy(0, group).start()
    for load in loads:
        load.wait()

    def head_cols(head):
        return pl.ds(pl.multiple_of(head * HD, HD), HD)

    def softmax(scores):
        top = jnp.max(scores, axis=0, keepdims=True)
        expo = jnp.exp2((scores - top) * SCALE2)
        return expo.astype(jnp.bfloat16), top * SCALE2, jnp.sum(expo, axis=0, keepdims=True)

    def own_group(group, _):
        tops, totals = [], []
        for j in range(GH):
            head = group * GH + j
            cols = head_cols(head)
            value_t = v[:, cols].T
            v_t[head] = value_t
            w_t[head] = w[cols, :].T
            scores = lax.dot_general(k[:, cols], q[:, cols], NT, preferred_element_type=jnp.float32)
            probs, top, total = softmax(scores)
            own[head] = jnp.dot(value_t, probs, preferred_element_type=jnp.float32)
            tops.append(top)
            totals.append(total)
        heads = pl.ds(pl.multiple_of(group * GH, GH), GH)
        stat_own[0, heads, :] = jnp.concatenate(tops, axis=0)
        stat_own[1, heads, :] = jnp.concatenate(totals, axis=0)
        return 0

    lax.fori_loop(0, COLG, own_group, 0)
    stat_copy = small_copy(stat_own, stat_in, 0)
    stat_copy.start()
    for group in range(COLG):
        query_copy(1, group).start()
    stat_copy.wait_recv()

    def share(top, total, top_b, total_b):
        most = jnp.maximum(top, top_b)
        mine = jnp.exp2(top - most)
        return mine / (total * mine + total_b * jnp.exp2(top_b - most))

    def partner_group(half, group, acc):
        rows = pl.ds(half * HALF, HALF)
        query_copy(half, group).wait_recv()
        first = group * GH if isinstance(group, int) else pl.multiple_of(group * GH, GH)
        heads = pl.ds(first, GH)
        tops_b = stat_in[0, heads, rows]
        totals_b = stat_in[1, heads, rows]
        tops, totals = [], []
        for j in range(GH):
            head = group * GH + j
            cols = head_cols(head)
            scores = lax.dot_general(
                k[:, cols], q_in[rows, cols], NT, preferred_element_type=jnp.float32
            )
            probs, top, total = softmax(scores)
            mixed = jnp.dot(v_t[head], probs, preferred_element_type=jnp.float32)
            part = share(top, total, tops_b[j : j + 1], totals_b[j : j + 1])
            acc = acc + jnp.dot(
                w_t[head], (mixed * part).astype(jnp.bfloat16), preferred_element_type=jnp.float32
            )
            tops.append(top)
            totals.append(total)
        ret[half, pl.ds(4 * LC + first, GH), :] = jnp.concatenate(tops, axis=0)
        ret[half, pl.ds(4 * LC + H + first, GH), :] = jnp.concatenate(totals, axis=0)
        return acc

    ret_copies = [small_copy(ret.at[half], ret_in.at[half], 1 + half) for half in range(2)]
    lat_copies = [small_copy(lat_own.at[half], lat_in.at[half], 3 + half) for half in range(2)]

    def send_ret(half, acc):
        ret[half, : 4 * LC, :] = acc
        ret_copies[half].start()

    def finish(half):
        rows = pl.ds(half * HALF, HALF)
        ret_copies[half].wait_recv()
        part = share(
            stat_own[0, :, rows],
            stat_own[1, :, rows],
            ret_in[half, 4 * LC : 4 * LC + H, :],
            ret_in[half, 4 * LC + H :, :],
        )
        acc = ret_in[half, : 4 * LC, :]
        for head in range(H):
            acc = acc + jnp.dot(
                w_t[head],
                (own[head, :, rows] * part[head : head + 1]).astype(jnp.bfloat16),
                preferred_element_type=jnp.float32,
            )
        lat_own[half] = acc.astype(jnp.bfloat16)
        lat_copies[half].start()
        lat_out[me, half] = lat_own[half]

    zero = jnp.zeros((4 * LC, HALF), jnp.float32)
    acc = lax.fori_loop(0, COLG, lambda g, a: partner_group(0, g, a), zero)
    send_ret(0, acc)
    acc = partner_group(1, 0, zero)
    finish(0)
    acc = lax.fori_loop(1, COLG, lambda g, a: partner_group(1, g, a), acc)
    send_ret(1, acc)
    finish(1)
    for half in range(2):
        lat_copies[half].wait_recv()
        lat_out[other, half] = lat_in[half]
    for half in range(2):
        for group in range(COLG):
            query_copy(half, group).wait_send()
    for copy in [stat_copy, *ret_copies, *lat_copies]:
        copy.wait_send()


def attend(queries, keys_in, values_in, latent_proj):
    width = H * HD
    any_spec = pl.BlockSpec(memory_space=pl.ANY)
    bf16, f32 = jnp.bfloat16, jnp.float32
    return pl.pallas_call(
        attend_kernel,
        out_shape=jax.ShapeDtypeStruct((2, 2, 4 * LC, HALF), bf16),
        in_specs=[any_spec] * 4,
        out_specs=pl.BlockSpec(memory_space=pltpu.VMEM),
        scratch_shapes=[
            pltpu.VMEM((S_DEV, width), bf16),
            pltpu.VMEM((S_DEV, width), bf16),
            pltpu.VMEM((S_DEV, width), bf16),
            pltpu.VMEM((width, 4 * LC), bf16),
            pltpu.VMEM((S_DEV, width), bf16),
            pltpu.VMEM((H, HD, S_DEV), bf16),
            pltpu.VMEM((H, 4 * LC, HD), bf16),
            pltpu.VMEM((H, HD, S_DEV), f32),
            pltpu.VMEM((2, H, S_DEV), f32),
            pltpu.VMEM((2, H, S_DEV), f32),
            pltpu.VMEM((2, 4 * LC + 2 * H, HALF), f32),
            pltpu.VMEM((2, 4 * LC + 2 * H, HALF), f32),
            pltpu.VMEM((2, 4 * LC, HALF), bf16),
            pltpu.VMEM((2, 4 * LC, HALF), bf16),
            pltpu.SemaphoreType.DMA((4,)),
            pltpu.SemaphoreType.DMA((2 * COLG,)),
            pltpu.SemaphoreType.DMA((2 * COLG,)),
            pltpu.SemaphoreType.DMA((5,)),
            pltpu.SemaphoreType.DMA((5,)),
        ],
        compiler_params=pltpu.CompilerParams(
            collective_id=0, has_side_effects=True, vmem_limit_bytes=56 * 2**20
        ),
    )(queries, keys_in, values_in, latent_proj)


def local_pair(
    queries,
    keys_in,
    values_in,
    latent_proj,
    conv_weight,
    conv_bias,
    pool_weight,
    tile_block,
    owner_slot,
):
    my_index = lax.axis_index("seq")
    lat = attend(queries, keys_in, values_in, latent_proj)
    tokens = lat.transpose(0, 1, 3, 2).reshape(8, S_DEV // 4, 4 * LC)
    blocks = picked(tokens, tile_block).reshape(2, FT, RT, WT, 2, 2, LC)
    video = blocks.transpose(1, 0, 2, 4, 3, 5, 6).reshape(FT, 2 * RL, COLS, LC)
    volume = jnp.pad(video, ((2, 0), (1, 1), (1, 1), (0, 0)))
    volume = lax.dynamic_slice_in_dim(volume, my_index * RL, RL + 2, axis=1)
    pre_act = (
        jnp.dot(window_columns(volume), conv_weight, preferred_element_type=jnp.float32) + conv_bias
    )
    decoded = pre_act.astype(jnp.bfloat16).reshape(1, FT, RL, COLS, CO)
    weighted = jax.nn.silu(pre_act).reshape(FT, RL, COLS, CO) * pool_weight[0][..., None]
    pooled_term = jnp.sum(weighted, axis=(0, 1)).reshape(4, COLS // 4, CO).sum(axis=1) / math.sqrt(
        2 * FT * RL * COLS // 4
    )
    total_pooled = lax.psum(pooled_term.astype(jnp.bfloat16), "seq").astype(jnp.float32)
    wanted_rows = my_index * BPD + jnp.arange(BPD, dtype=jnp.int32)
    chooser = (owner_slot[None, :] == wanted_rows[:, None]).astype(jnp.float32)
    policy = jnp.dot(
        chooser, total_pooled, precision=lax.Precision.HIGHEST, preferred_element_type=jnp.float32
    )
    return (decoded, policy)


def solution(mesh):
    placed = (
        P(("roll", "seq"), None),
        P(("roll", "seq"), None),
        P(("roll", "seq"), None),
        P(),
        P(),
        P(),
        P("seq", None, None, None),
        P("roll"),
        P("roll"),
    )
    return jax.shard_map(
        local_pair if mesh.shape["seq"] == 2 else local_any,
        mesh=mesh,
        in_specs=placed,
        out_specs=(P(("roll", "seq"), None, None, None, None), P(("roll", "seq"), None)),
        check_vma=False,
    )
```

```python
import math

import jax
import jax.numpy as jnp
from jax import lax
from jax.experimental import pallas as pl
from jax.experimental.pallas import tpu as pltpu
from jax.sharding import PartitionSpec as P

H = 24
HD = 128
LC = 16
CO = 512
S_DEV = 256
RT = 4
WT = 32
TR = 2
BPD = 2
FT = 2
RL = 8
COLS = 64


def shifted(array, axis, by):
    length = lax.axis_size(axis)
    pairs = [(i, i + by) for i in range(length) if 0 <= i + by < length]
    return lax.ppermute(array, axis, pairs)


def swapped(array, axis, bit):
    return lax.ppermute(array, axis, [(i, i ^ 1 << bit) for i in range(lax.axis_size(axis))])


def heads_attention(query_all, key_all, value_all):
    length = query_all.shape[0]
    block_rows = min(512, length)
    score_scale = 1.0 / math.sqrt(query_all.shape[2])
    query_blocks = query_all.reshape(
        length // block_rows, block_rows, query_all.shape[1], query_all.shape[2]
    )

    def one_block(query_part):
        scores = (
            jnp.einsum("qhd,khd->hqk", query_part, key_all, preferred_element_type=jnp.float32)
            * score_scale
        )
        expo = jnp.exp(scores - jnp.max(scores, axis=-1, keepdims=True))
        totals = jnp.sum(expo, axis=-1, keepdims=True)
        mixed = jnp.einsum(
            "hqk,khd->qhd", expo.astype(jnp.bfloat16), value_all, preferred_element_type=jnp.float32
        )
        return (mixed / jnp.transpose(totals, (1, 0, 2))).astype(jnp.bfloat16)

    return lax.map(one_block, query_blocks).reshape(length, query_all.shape[1], query_all.shape[2])


def window_columns(volume):
    frame_count = volume.shape[0] - 2
    row_count = volume.shape[1] - 2
    col_count = volume.shape[2] - 2
    pieces = [
        volume[a : a + frame_count, b : b + row_count, c : c + col_count]
        for a in range(3)
        for b in range(3)
        for c in range(3)
    ]
    return jnp.concatenate(pieces, axis=-1).reshape(
        frame_count * row_count * col_count, 27 * volume.shape[3]
    )


def picked(blocks, order):
    count = blocks.shape[0]
    choose = (order[:, None] == jnp.arange(count, dtype=jnp.int32)[None, :]).astype(jnp.bfloat16)
    flat = jnp.dot(choose, blocks.reshape(count, -1), preferred_element_type=jnp.float32)
    return flat.astype(jnp.bfloat16).reshape(blocks.shape)


def local_any(
    queries,
    keys_in,
    values_in,
    latent_proj,
    conv_weight,
    conv_bias,
    pool_weight,
    tile_block,
    owner_slot,
):
    group_count = lax.axis_size("seq")
    my_index = lax.axis_index("seq")
    seq_len = S_DEV * group_count
    heads_dev = H // group_count
    quarter = S_DEV // 4

    def to_groups(matrix):
        return matrix.reshape(S_DEV, group_count, heads_dev, HD)

    query_all = lax.all_to_all(to_groups(queries), "seq", split_axis=1, concat_axis=0, tiled=True)
    key_all = lax.all_to_all(to_groups(keys_in), "seq", split_axis=1, concat_axis=0, tiled=True)
    value_all = lax.all_to_all(to_groups(values_in), "seq", split_axis=1, concat_axis=0, tiled=True)
    mixed = heads_attention(query_all[:, 0], key_all[:, 0], value_all[:, 0])[:, None]
    flat_heads = mixed.reshape(seq_len, heads_dev * HD)
    ordered = picked(flat_heads.reshape(4 * group_count, quarter, heads_dev * HD), tile_block)
    ordered = ordered.reshape(seq_len, 1, heads_dev, HD)
    returned = lax.all_to_all(ordered, "seq", split_axis=0, concat_axis=1, tiled=True)
    tile_heads = returned.reshape(S_DEV, H * HD)
    latent = jnp.dot(tile_heads, latent_proj, preferred_element_type=jnp.float32).astype(
        jnp.bfloat16
    )
    tile_latent = (
        latent.reshape(FT, RT, WT, 2, 2, LC).transpose(0, 1, 3, 2, 4, 5).reshape(FT, RL, COLS * LC)
    )
    earlier = shifted(tile_latent, "seq", TR)
    extended = jnp.concatenate([earlier, tile_latent], axis=0)
    band_row = my_index % TR
    upper_band = band_row == 0
    outgoing = jnp.where(upper_band, extended[:, RL - 1 :], extended[:, :1])
    incoming = swapped(outgoing, "seq", 0)
    above = jnp.where(upper_band, jnp.zeros_like(incoming), incoming)
    below = jnp.where(upper_band, incoming, jnp.zeros_like(incoming))
    volume = jnp.concatenate([above, extended, below], axis=1).reshape(FT + 2, RL + 2, COLS, LC)
    volume = jnp.pad(volume, ((0, 0), (0, 0), (1, 1), (0, 0)))
    pre_act = (
        jnp.dot(window_columns(volume), conv_weight, preferred_element_type=jnp.float32) + conv_bias
    )
    decoded = pre_act.astype(jnp.bfloat16).reshape(1, FT, RL, COLS, CO)
    block_count = BPD * group_count
    band_voxels = group_count // TR * FT * TR * RL * (COLS // block_count)
    weighted = jax.nn.silu(pre_act).reshape(FT, RL, COLS, CO) * pool_weight[0][..., None]
    pooled_term = jnp.sum(weighted, axis=(0, 1)).reshape(block_count, COLS // block_count, CO).sum(
        axis=1
    ) / math.sqrt(band_voxels)
    total_pooled = lax.psum(pooled_term.astype(jnp.bfloat16), "seq").astype(jnp.float32)
    wanted_rows = my_index * BPD + jnp.arange(BPD, dtype=jnp.int32)
    chooser = (owner_slot[None, :] == wanted_rows[:, None]).astype(jnp.float32)
    policy = jnp.dot(
        chooser, total_pooled, precision=lax.Precision.HIGHEST, preferred_element_type=jnp.float32
    )
    return (decoded, policy)


SCALE2 = math.log2(math.e) / math.sqrt(HD)
HALF = S_DEV // 2
COLG = 3
GH = H // COLG
GW = GH * HD
NT = (((1,), (1,)), ((), ()))


def attend_kernel(
    q_hbm,
    k_hbm,
    v_hbm,
    w_hbm,
    pool,
    lat_out,
    pool_out,
    q,
    k,
    v,
    w,
    q_in,
    v_t,
    w_t,
    own,
    stat_own,
    stat_in,
    ret,
    ret_in,
    lat_own,
    lat_in,
    pool_in,
    load_sem,
    q_send,
    q_recv,
    small_send,
    small_recv,
):
    me = lax.axis_index("seq")
    other = 1 - me
    loads = [
        pltpu.make_async_copy(src, dst, load_sem.at[i])
        for i, (src, dst) in enumerate(((q_hbm, q), (k_hbm, k), (v_hbm, v), (w_hbm, w)))
    ]
    for load in loads:
        load.start()

    barrier = pltpu.get_barrier_semaphore()
    pl.semaphore_signal(barrier, inc=1, device_id={"seq": other})
    pl.semaphore_wait(barrier, 1)

    def query_copy(half, group):
        rows = pl.ds(half * HALF, HALF)
        start = group * GW
        if not isinstance(group, int):
            start = pl.multiple_of(start, GW)
        part = (rows, pl.ds(start, GW))
        return pltpu.make_async_remote_copy(
            src_ref=q_hbm.at[part],
            dst_ref=q_in.at[part],
            send_sem=q_send.at[half * COLG + group],
            recv_sem=q_recv.at[half * COLG + group],
            device_id={"seq": other},
        )

    def small_copy(src, dst, slot):
        return pltpu.make_async_remote_copy(
            src_ref=src,
            dst_ref=dst,
            send_sem=small_send.at[slot],
            recv_sem=small_recv.at[slot],
            device_id={"seq": other},
        )

    for group in range(COLG):
        query_copy(0, group).start()
    for load in loads:
        load.wait()

    def head_cols(head):
        return pl.ds(pl.multiple_of(head * HD, HD), HD)

    def softmax(scores):
        top = jnp.max(scores, axis=0, keepdims=True)
        expo = jnp.exp2((scores - top) * SCALE2)
        return expo.astype(jnp.bfloat16), top * SCALE2, jnp.sum(expo, axis=0, keepdims=True)

    def own_group(group, _):
        tops, totals = [], []
        for j in range(GH):
            head = group * GH + j
            cols = head_cols(head)
            value_t = v[:, cols].T
            v_t[head] = value_t
            w_t[head] = w[:, cols]
            scores = lax.dot_general(k[:, cols], q[:, cols], NT, preferred_element_type=jnp.float32)
            probs, top, total = softmax(scores)
            own[head] = jnp.dot(value_t, probs, preferred_element_type=jnp.float32)
            tops.append(top)
            totals.append(total)
        heads = pl.ds(pl.multiple_of(group * GH, GH), GH)
        stat_own[0, heads, :] = jnp.concatenate(tops, axis=0)
        stat_own[1, heads, :] = jnp.concatenate(totals, axis=0)
        return 0

    lax.fori_loop(0, COLG, own_group, 0)
    stat_copy = small_copy(stat_own, stat_in, 0)
    stat_copy.start()
    pool_copy = small_copy(pool, pool_in, 5)
    pool_copy.start()
    pool_out[me] = pool[...]
    for group in range(COLG):
        query_copy(1, group).start()
    stat_copy.wait_recv()

    def share(top, total, top_b, total_b):
        most = jnp.maximum(top, top_b)
        mine = jnp.exp2(top - most)
        return mine / (total * mine + total_b * jnp.exp2(top_b - most))

    def partner_group(half, group, acc):
        rows = pl.ds(half * HALF, HALF)
        query_copy(half, group).wait_recv()
        first = group * GH if isinstance(group, int) else pl.multiple_of(group * GH, GH)
        heads = pl.ds(first, GH)
        tops_b = stat_in[0, heads, rows]
        totals_b = stat_in[1, heads, rows]
        tops, totals = [], []
        for j in range(GH):
            head = group * GH + j
            cols = head_cols(head)
            scores = lax.dot_general(
                k[:, cols], q_in[rows, cols], NT, preferred_element_type=jnp.float32
            )
            probs, top, total = softmax(scores)
            mixed = jnp.dot(v_t[head], probs, preferred_element_type=jnp.float32)
            part = share(top, total, tops_b[j : j + 1], totals_b[j : j + 1])
            acc = acc + jnp.dot(
                w_t[head], (mixed * part).astype(jnp.bfloat16), preferred_element_type=jnp.float32
            )
            tops.append(top)
            totals.append(total)
        ret[half, pl.ds(4 * LC + first, GH), :] = jnp.concatenate(tops, axis=0)
        ret[half, pl.ds(4 * LC + H + first, GH), :] = jnp.concatenate(totals, axis=0)
        return acc

    ret_copies = [small_copy(ret.at[half], ret_in.at[half], 1 + half) for half in range(2)]
    lat_copies = [small_copy(lat_own.at[half], lat_in.at[half], 3 + half) for half in range(2)]

    def send_ret(half, acc):
        ret[half, : 4 * LC, :] = acc
        ret_copies[half].start()

    def finish(half):
        rows = pl.ds(half * HALF, HALF)
        ret_copies[half].wait_recv()
        part = share(
            stat_own[0, :, rows],
            stat_own[1, :, rows],
            ret_in[half, 4 * LC : 4 * LC + H, :],
            ret_in[half, 4 * LC + H :, :],
        )
        acc = ret_in[half, : 4 * LC, :]
        for head in range(H):
            acc = acc + jnp.dot(
                w_t[head],
                (own[head, :, rows] * part[head : head + 1]).astype(jnp.bfloat16),
                preferred_element_type=jnp.float32,
            )
        lat_own[half] = acc.astype(jnp.bfloat16)
        lat_copies[half].start()
        lat_out[me, half] = lat_own[half]

    zero = jnp.zeros((4 * LC, HALF), jnp.float32)
    acc = lax.fori_loop(0, COLG, lambda g, a: partner_group(0, g, a), zero)
    send_ret(0, acc)
    acc = partner_group(1, 0, zero)
    finish(0)
    acc = lax.fori_loop(1, COLG, lambda g, a: partner_group(1, g, a), acc)
    send_ret(1, acc)
    finish(1)
    pool_copy.wait_recv()
    pool_out[other] = pool_in[...]
    for half in range(2):
        lat_copies[half].wait_recv()
        lat_out[other, half] = lat_in[half]
    for half in range(2):
        for group in range(COLG):
            query_copy(half, group).wait_send()
    for copy in [stat_copy, pool_copy, *ret_copies, *lat_copies]:
        copy.wait_send()


def attend(queries, keys_in, values_in, latent_proj, pool_weight):
    width = H * HD
    any_spec = pl.BlockSpec(memory_space=pl.ANY)
    bf16, f32 = jnp.bfloat16, jnp.float32
    return pl.pallas_call(
        attend_kernel,
        out_shape=[
            jax.ShapeDtypeStruct((2, 2, 4 * LC, HALF), bf16),
            jax.ShapeDtypeStruct((2, 8, HALF), f32),
        ],
        in_specs=[any_spec] * 4 + [pl.BlockSpec(memory_space=pltpu.VMEM)],
        out_specs=[pl.BlockSpec(memory_space=pltpu.VMEM)] * 2,
        scratch_shapes=[
            pltpu.VMEM((S_DEV, width), bf16),
            pltpu.VMEM((S_DEV, width), bf16),
            pltpu.VMEM((S_DEV, width), bf16),
            pltpu.VMEM((4 * LC, width), bf16),
            pltpu.VMEM((S_DEV, width), bf16),
            pltpu.VMEM((H, HD, S_DEV), bf16),
            pltpu.VMEM((H, 4 * LC, HD), bf16),
            pltpu.VMEM((H, HD, S_DEV), f32),
            pltpu.VMEM((2, H, S_DEV), f32),
            pltpu.VMEM((2, H, S_DEV), f32),
            pltpu.VMEM((2, 4 * LC + 2 * H, HALF), f32),
            pltpu.VMEM((2, 4 * LC + 2 * H, HALF), f32),
            pltpu.VMEM((2, 4 * LC, HALF), bf16),
            pltpu.VMEM((2, 4 * LC, HALF), bf16),
            pltpu.VMEM((8, HALF), f32),
            pltpu.SemaphoreType.DMA((4,)),
            pltpu.SemaphoreType.DMA((2 * COLG,)),
            pltpu.SemaphoreType.DMA((2 * COLG,)),
            pltpu.SemaphoreType.DMA((6,)),
            pltpu.SemaphoreType.DMA((6,)),
        ],
        compiler_params=pltpu.CompilerParams(
            collective_id=0, has_side_effects=True, vmem_limit_bytes=56 * 2**20
        ),
    )(queries, keys_in, values_in, latent_proj.T, pool_weight.reshape(8, HALF))


def decode_kernel(
    lat, weight, bias, pool, tile_block, owner_slot, dec_hbm, policy, tok, vol, patch, dec, sem
):
    me = lax.axis_index("seq")
    f32, bf16 = jnp.float32, jnp.bfloat16
    for part in range(2):
        for half in range(2):
            first = (part * 2 + half) * HALF
            tok[first : first + HALF, :] = lat[part, half].astype(f32).T

    rows, width = 2 * RL, 3 * LC
    vol[:, :1] = jnp.zeros((FT, 1, COLS + 16, LC), f32)
    vol[:, rows + 1 :] = jnp.zeros((FT, 1, COLS + 16, LC), f32)
    vol[:, :, :8] = jnp.zeros((FT, rows + 2, 8, LC), f32)
    vol[:, :, COLS + 8 :] = jnp.zeros((FT, rows + 2, 8, LC), f32)
    patch[:2] = jnp.zeros((2, rows, COLS, 3 * width), bf16)
    for place in range(8):
        tile, frame, pair = place // 4, place // 2 % 2, place % 2
        first = tile_block[place] * (2 * WT)
        for j in range(2):
            values = tok[pl.ds(pl.multiple_of(first + j * WT, WT), WT), :]
            for dy in range(2):
                row = 1 + tile * RL + (pair * 2 + j) * 2 + dy
                for dx in range(2):
                    lanes = (dy * 2 + dx) * LC
                    vol[frame, row, pl.ds(8 + dx, WT, stride=2), :] = values[:, lanes : lanes + LC]

    for frame in range(FT):
        spans = []
        for row in range(rows + 2):
            spans.append(
                jnp.concatenate(
                    [vol[frame, row, 7 + c : 7 + c + COLS, :] for c in range(3)], axis=-1
                ).astype(bf16)
            )
        for row in range(rows):
            patch[frame + 2, row] = jnp.concatenate(spans[row : row + 3], axis=-1)

    lane = lax.broadcasted_iota(jnp.int32, (8, RL * COLS), 1)
    line = lax.broadcasted_iota(jnp.int32, (8, RL * COLS), 0)
    in_band = (lane % COLS) // (COLS // 4) == line % 4
    high_line = line < 4
    pooled = jnp.zeros((8, CO), f32)
    out_copy = pltpu.make_async_copy(dec, dec_hbm, sem)
    for turn in range(2):
        tile = me if turn == 0 else 1 - me
        tile_rows = pl.ds(pl.multiple_of(tile * RL, RL), RL)
        for frame in range(FT):
            pre = bias[...]
            for a in range(3):
                pre = pre + jnp.dot(
                    patch[frame + a, tile_rows].reshape(RL * COLS, 3 * width),
                    weight[a * 3 * width : (a + 1) * 3 * width, :],
                    preferred_element_type=f32,
                )
            if turn == 0:
                dec[0, frame] = pre.astype(bf16).reshape(RL, COLS, CO)
            act = (0.5 * pre) * (1.0 + jnp.tanh(0.5 * pre))
            own = jnp.concatenate(
                [pool[tile, frame * 4 + i : frame * 4 + i + 1, :] for i in range(4)], axis=-1
            )
            high = own.astype(bf16).astype(f32)
            terms = jnp.where(in_band, jnp.where(high_line, high, own - high), 0.0)
            pooled = pooled + jnp.dot(
                terms.astype(bf16), act.astype(bf16), preferred_element_type=f32
            )
        if turn == 0:
            out_copy.start()
    total = (pooled[:4] + pooled[4:]) * (1.0 / math.sqrt(2 * FT * RL * COLS // 4))
    for i in range(BPD):
        line_out = jnp.zeros((1, CO), f32)
        for band in range(4):
            line_out = jnp.where(owner_slot[band] == me * BPD + i, total[band : band + 1], line_out)
        policy[i : i + 1, :] = line_out
    out_copy.wait()


def decode(lat, conv_weight, conv_bias, pool, tile_block, owner_slot):
    vmem = pl.BlockSpec(memory_space=pltpu.VMEM)
    smem = pl.BlockSpec(memory_space=pltpu.SMEM)
    bf16, f32 = jnp.bfloat16, jnp.float32
    dec_shape = (1, FT, RL, COLS, CO)
    return pl.pallas_call(
        decode_kernel,
        out_shape=[jax.ShapeDtypeStruct(dec_shape, bf16), jax.ShapeDtypeStruct((BPD, CO), f32)],
        in_specs=[vmem] * 4 + [smem] * 2,
        out_specs=[pl.BlockSpec(memory_space=pl.ANY), vmem],
        scratch_shapes=[
            pltpu.VMEM((2 * S_DEV, 4 * LC), f32),
            pltpu.VMEM((FT, 2 * RL + 2, COLS + 16, LC), f32),
            pltpu.VMEM((FT + 2, 2 * RL, COLS, 9 * LC), bf16),
            pltpu.VMEM(dec_shape, bf16),
            pltpu.SemaphoreType.DMA,
        ],
        compiler_params=pltpu.CompilerParams(vmem_limit_bytes=48 * 2**20),
    )(lat, conv_weight, conv_bias.reshape(1, CO), pool, tile_block, owner_slot)


def local_pair(
    queries,
    keys_in,
    values_in,
    latent_proj,
    conv_weight,
    conv_bias,
    pool_weight,
    tile_block,
    owner_slot,
):
    lat, pool = attend(queries, keys_in, values_in, latent_proj, pool_weight)
    decoded, policy = decode(lat, conv_weight, conv_bias, pool, tile_block, owner_slot)
    return (decoded, policy)


def solution(mesh):
    placed = (
        P(("roll", "seq"), None),
        P(("roll", "seq"), None),
        P(("roll", "seq"), None),
        P(),
        P(),
        P(),
        P("seq", None, None, None),
        P("roll"),
        P("roll"),
    )
    return jax.shard_map(
        local_pair if mesh.shape["seq"] == 2 else local_any,
        mesh=mesh,
        in_specs=placed,
        out_specs=(P(("roll", "seq"), None, None, None, None), P(("roll", "seq"), None)),
        check_vma=False,
    )
```

```python
import math

import jax
import jax.numpy as jnp
from jax import lax
from jax.experimental import pallas as pl
from jax.experimental.pallas import tpu as pltpu
from jax.sharding import PartitionSpec as P

H = 24
HD = 128
LC = 16
CO = 512
S_DEV = 256
RT = 4
WT = 32
TR = 2
BPD = 2
FT = 2
RL = 8
COLS = 64


def shifted(array, axis, by):
    length = lax.axis_size(axis)
    pairs = [(i, i + by) for i in range(length) if 0 <= i + by < length]
    return lax.ppermute(array, axis, pairs)


def swapped(array, axis, bit):
    return lax.ppermute(array, axis, [(i, i ^ 1 << bit) for i in range(lax.axis_size(axis))])


def heads_attention(query_all, key_all, value_all):
    length = query_all.shape[0]
    block_rows = min(512, length)
    score_scale = 1.0 / math.sqrt(query_all.shape[2])
    query_blocks = query_all.reshape(
        length // block_rows, block_rows, query_all.shape[1], query_all.shape[2]
    )

    def one_block(query_part):
        scores = (
            jnp.einsum("qhd,khd->hqk", query_part, key_all, preferred_element_type=jnp.float32)
            * score_scale
        )
        expo = jnp.exp(scores - jnp.max(scores, axis=-1, keepdims=True))
        totals = jnp.sum(expo, axis=-1, keepdims=True)
        mixed = jnp.einsum(
            "hqk,khd->qhd", expo.astype(jnp.bfloat16), value_all, preferred_element_type=jnp.float32
        )
        return (mixed / jnp.transpose(totals, (1, 0, 2))).astype(jnp.bfloat16)

    return lax.map(one_block, query_blocks).reshape(length, query_all.shape[1], query_all.shape[2])


def window_columns(volume):
    frame_count = volume.shape[0] - 2
    row_count = volume.shape[1] - 2
    col_count = volume.shape[2] - 2
    pieces = [
        volume[a : a + frame_count, b : b + row_count, c : c + col_count]
        for a in range(3)
        for b in range(3)
        for c in range(3)
    ]
    return jnp.concatenate(pieces, axis=-1).reshape(
        frame_count * row_count * col_count, 27 * volume.shape[3]
    )


def picked(blocks, order):
    count = blocks.shape[0]
    choose = (order[:, None] == jnp.arange(count, dtype=jnp.int32)[None, :]).astype(jnp.bfloat16)
    flat = jnp.dot(choose, blocks.reshape(count, -1), preferred_element_type=jnp.float32)
    return flat.astype(jnp.bfloat16).reshape(blocks.shape)


def local_any(
    queries,
    keys_in,
    values_in,
    latent_proj,
    conv_weight,
    conv_bias,
    pool_weight,
    tile_block,
    owner_slot,
):
    group_count = lax.axis_size("seq")
    my_index = lax.axis_index("seq")
    seq_len = S_DEV * group_count
    heads_dev = H // group_count
    quarter = S_DEV // 4

    def to_groups(matrix):
        return matrix.reshape(S_DEV, group_count, heads_dev, HD)

    query_all = lax.all_to_all(to_groups(queries), "seq", split_axis=1, concat_axis=0, tiled=True)
    key_all = lax.all_to_all(to_groups(keys_in), "seq", split_axis=1, concat_axis=0, tiled=True)
    value_all = lax.all_to_all(to_groups(values_in), "seq", split_axis=1, concat_axis=0, tiled=True)
    mixed = heads_attention(query_all[:, 0], key_all[:, 0], value_all[:, 0])[:, None]
    flat_heads = mixed.reshape(seq_len, heads_dev * HD)
    ordered = picked(flat_heads.reshape(4 * group_count, quarter, heads_dev * HD), tile_block)
    ordered = ordered.reshape(seq_len, 1, heads_dev, HD)
    returned = lax.all_to_all(ordered, "seq", split_axis=0, concat_axis=1, tiled=True)
    tile_heads = returned.reshape(S_DEV, H * HD)
    latent = jnp.dot(tile_heads, latent_proj, preferred_element_type=jnp.float32).astype(
        jnp.bfloat16
    )
    tile_latent = (
        latent.reshape(FT, RT, WT, 2, 2, LC).transpose(0, 1, 3, 2, 4, 5).reshape(FT, RL, COLS * LC)
    )
    earlier = shifted(tile_latent, "seq", TR)
    extended = jnp.concatenate([earlier, tile_latent], axis=0)
    band_row = my_index % TR
    upper_band = band_row == 0
    outgoing = jnp.where(upper_band, extended[:, RL - 1 :], extended[:, :1])
    incoming = swapped(outgoing, "seq", 0)
    above = jnp.where(upper_band, jnp.zeros_like(incoming), incoming)
    below = jnp.where(upper_band, incoming, jnp.zeros_like(incoming))
    volume = jnp.concatenate([above, extended, below], axis=1).reshape(FT + 2, RL + 2, COLS, LC)
    volume = jnp.pad(volume, ((0, 0), (0, 0), (1, 1), (0, 0)))
    pre_act = (
        jnp.dot(window_columns(volume), conv_weight, preferred_element_type=jnp.float32) + conv_bias
    )
    decoded = pre_act.astype(jnp.bfloat16).reshape(1, FT, RL, COLS, CO)
    block_count = BPD * group_count
    band_voxels = group_count // TR * FT * TR * RL * (COLS // block_count)
    weighted = jax.nn.silu(pre_act).reshape(FT, RL, COLS, CO) * pool_weight[0][..., None]
    pooled_term = jnp.sum(weighted, axis=(0, 1)).reshape(block_count, COLS // block_count, CO).sum(
        axis=1
    ) / math.sqrt(band_voxels)
    total_pooled = lax.psum(pooled_term.astype(jnp.bfloat16), "seq").astype(jnp.float32)
    wanted_rows = my_index * BPD + jnp.arange(BPD, dtype=jnp.int32)
    chooser = (owner_slot[None, :] == wanted_rows[:, None]).astype(jnp.float32)
    policy = jnp.dot(
        chooser, total_pooled, precision=lax.Precision.HIGHEST, preferred_element_type=jnp.float32
    )
    return (decoded, policy)


SCALE2 = math.log2(math.e) / math.sqrt(HD)
HALF = S_DEV // 2
COLG = 3
GH = H // COLG
GW = GH * HD
NT = (((1,), (1,)), ((), ()))


def attend_kernel(
    q_hbm,
    k_hbm,
    v_hbm,
    w_hbm,
    pool,
    lat_out,
    pool_out,
    q,
    k,
    v,
    w,
    q_in,
    v_t,
    w_t,
    own,
    top_own,
    stat_own,
    stat_in,
    ret,
    ret_in,
    ret_level,
    level_in,
    lat_own,
    lat_in,
    pool_in,
    load_sem,
    q_send,
    q_recv,
    small_send,
    small_recv,
):
    me = lax.axis_index("seq")
    other = 1 - me
    loads = [
        pltpu.make_async_copy(src, dst, load_sem.at[i])
        for i, (src, dst) in enumerate(((q_hbm, q), (k_hbm, k), (v_hbm, v), (w_hbm, w)))
    ]
    for load in loads:
        load.start()

    barrier = pltpu.get_barrier_semaphore()
    pl.semaphore_signal(barrier, inc=1, device_id={"seq": other})
    pl.semaphore_wait(barrier, 1)

    def query_copy(half, group):
        rows = pl.ds(half * HALF, HALF)
        start = group * GW
        if not isinstance(group, int):
            start = pl.multiple_of(start, GW)
        part = (rows, pl.ds(start, GW))
        return pltpu.make_async_remote_copy(
            src_ref=q_hbm.at[part],
            dst_ref=q_in.at[part],
            send_sem=q_send.at[half * COLG + group],
            recv_sem=q_recv.at[half * COLG + group],
            device_id={"seq": other},
        )

    def small_copy(src, dst, slot):
        return pltpu.make_async_remote_copy(
            src_ref=src,
            dst_ref=dst,
            send_sem=small_send.at[slot],
            recv_sem=small_recv.at[slot],
            device_id={"seq": other},
        )

    for group in range(COLG):
        query_copy(0, group).start()
    for load in loads:
        load.wait()

    def head_cols(head):
        return pl.ds(pl.multiple_of(head * HD, HD), HD)

    def softmax(scores):
        top = jnp.max(scores, axis=0, keepdims=True)
        expo = jnp.exp2((scores - top) * SCALE2)
        top = top * SCALE2
        level = top + jnp.log(jnp.sum(expo, axis=0, keepdims=True)) * math.log2(math.e)
        return expo.astype(jnp.bfloat16), top, level

    def own_group(group, _):
        tops, levels = [], []
        for j in range(GH):
            head = group * GH + j
            cols = head_cols(head)
            value_t = v[:, cols].T
            v_t[head] = value_t
            w_t[head] = w[:, cols]
            scores = lax.dot_general(k[:, cols], q[:, cols], NT, preferred_element_type=jnp.float32)
            probs, top, level = softmax(scores)
            own[head] = jnp.dot(value_t, probs, preferred_element_type=jnp.float32)
            tops.append(top)
            levels.append(level)
        heads = pl.ds(pl.multiple_of(group * GH, GH), GH)
        top_own[heads, :] = jnp.concatenate(tops, axis=0)
        stat_own[heads, :] = jnp.concatenate(levels, axis=0)
        return 0

    lax.fori_loop(0, COLG, own_group, 0)
    stat_copy = small_copy(stat_own, stat_in, 0)
    stat_copy.start()
    pool_copy = small_copy(pool, pool_in, 5)
    pool_copy.start()
    pool_out[me] = pool[...]
    for group in range(COLG):
        query_copy(1, group).start()
    stat_copy.wait_recv()

    def share(top, level, level_b):
        most = jnp.maximum(level, level_b)
        both = jnp.exp2(level - most) + jnp.exp2(level_b - most)
        return jnp.exp2(top - most) / both

    def partner_group(half, group, acc):
        rows = pl.ds(half * HALF, HALF)
        query_copy(half, group).wait_recv()
        first = group * GH if isinstance(group, int) else pl.multiple_of(group * GH, GH)
        heads = pl.ds(first, GH)
        levels_b = stat_in[heads, rows]
        levels = []
        for j in range(GH):
            head = group * GH + j
            cols = head_cols(head)
            scores = lax.dot_general(
                k[:, cols], q_in[rows, cols], NT, preferred_element_type=jnp.float32
            )
            probs, top, level = softmax(scores)
            mixed = jnp.dot(v_t[head], probs, preferred_element_type=jnp.float32)
            part = share(top, level, levels_b[j : j + 1])
            acc = acc + jnp.dot(
                w_t[head], (mixed * part).astype(jnp.bfloat16), preferred_element_type=jnp.float32
            )
            levels.append(level)
        ret_level[half, heads, :] = jnp.concatenate(levels, axis=0)
        return acc

    ret_copies = [small_copy(ret.at[half], ret_in.at[half], 1 + half) for half in range(2)]
    level_copies = [
        small_copy(ret_level.at[half], level_in.at[half], 6 + half) for half in range(2)
    ]
    lat_copies = [small_copy(lat_own.at[half], lat_in.at[half], 3 + half) for half in range(2)]

    def send_ret(half, acc):
        level_copies[half].start()
        ret[half] = acc.astype(jnp.bfloat16)
        ret_copies[half].start()

    def finish(half):
        rows = pl.ds(half * HALF, HALF)
        level_copies[half].wait_recv()
        part = share(top_own[:, rows], stat_own[:, rows], level_in[half])
        ret_copies[half].wait_recv()
        acc = ret_in[half].astype(jnp.float32)
        for head in range(H):
            acc = acc + jnp.dot(
                w_t[head],
                (own[head, :, rows] * part[head : head + 1]).astype(jnp.bfloat16),
                preferred_element_type=jnp.float32,
            )
        lat_own[half] = acc.astype(jnp.bfloat16)
        lat_copies[half].start()
        lat_out[me, half] = lat_own[half]

    zero = jnp.zeros((4 * LC, HALF), jnp.float32)
    acc = lax.fori_loop(0, COLG, lambda g, a: partner_group(0, g, a), zero)
    send_ret(0, acc)
    acc = partner_group(1, 0, zero)
    finish(0)
    acc = lax.fori_loop(1, COLG, lambda g, a: partner_group(1, g, a), acc)
    send_ret(1, acc)
    finish(1)
    pool_copy.wait_recv()
    pool_out[other] = pool_in[...]
    for half in range(2):
        lat_copies[half].wait_recv()
        lat_out[other, half] = lat_in[half]
    for half in range(2):
        for group in range(COLG):
            query_copy(half, group).wait_send()
    for copy in [stat_copy, pool_copy, *level_copies, *ret_copies, *lat_copies]:
        copy.wait_send()


def attend(queries, keys_in, values_in, latent_proj, pool_weight):
    width = H * HD
    any_spec = pl.BlockSpec(memory_space=pl.ANY)
    bf16, f32 = jnp.bfloat16, jnp.float32
    return pl.pallas_call(
        attend_kernel,
        out_shape=[
            jax.ShapeDtypeStruct((2, 2, 4 * LC, HALF), bf16),
            jax.ShapeDtypeStruct((2, FT * RL, COLS), f32),
        ],
        in_specs=[any_spec] * 4 + [pl.BlockSpec(memory_space=pltpu.VMEM)],
        out_specs=[pl.BlockSpec(memory_space=pltpu.VMEM)] * 2,
        scratch_shapes=[
            pltpu.VMEM((S_DEV, width), bf16),
            pltpu.VMEM((S_DEV, width), bf16),
            pltpu.VMEM((S_DEV, width), bf16),
            pltpu.VMEM((4 * LC, width), bf16),
            pltpu.VMEM((S_DEV, width), bf16),
            pltpu.VMEM((H, HD, S_DEV), bf16),
            pltpu.VMEM((H, 4 * LC, HD), bf16),
            pltpu.VMEM((H, HD, S_DEV), f32),
            pltpu.VMEM((H, S_DEV), f32),
            pltpu.VMEM((H, S_DEV), f32),
            pltpu.VMEM((H, S_DEV), f32),
            pltpu.VMEM((2, 4 * LC, HALF), bf16),
            pltpu.VMEM((2, 4 * LC, HALF), bf16),
            pltpu.VMEM((2, H, HALF), f32),
            pltpu.VMEM((2, H, HALF), f32),
            pltpu.VMEM((2, 4 * LC, HALF), bf16),
            pltpu.VMEM((2, 4 * LC, HALF), bf16),
            pltpu.VMEM((FT * RL, COLS), f32),
            pltpu.SemaphoreType.DMA((4,)),
            pltpu.SemaphoreType.DMA((2 * COLG,)),
            pltpu.SemaphoreType.DMA((2 * COLG,)),
            pltpu.SemaphoreType.DMA((8,)),
            pltpu.SemaphoreType.DMA((8,)),
        ],
        compiler_params=pltpu.CompilerParams(
            collective_id=0, has_side_effects=True, vmem_limit_bytes=56 * 2**20
        ),
    )(queries, keys_in, values_in, latent_proj.T, pool_weight.reshape(FT * RL, COLS))


def decode_kernel(
    lat, weight, bias, pool, tile_block, owner_slot, dec_hbm, policy, tok, vol, patch, dec, sem
):
    me = lax.axis_index("seq")
    f32, bf16 = jnp.float32, jnp.bfloat16
    for part in range(2):
        for half in range(2):
            first = (part * 2 + half) * HALF
            tok[first : first + HALF, :] = lat[part, half].astype(f32).T

    rows, width = 2 * RL, 3 * LC
    vol[:, :1] = jnp.zeros((FT, 1, COLS + 16, LC), f32)
    vol[:, rows + 1 :] = jnp.zeros((FT, 1, COLS + 16, LC), f32)
    vol[:, :, :8] = jnp.zeros((FT, rows + 2, 8, LC), f32)
    vol[:, :, COLS + 8 :] = jnp.zeros((FT, rows + 2, 8, LC), f32)
    patch[:2] = jnp.zeros((2, rows, COLS, 3 * width), bf16)
    for place in range(8):
        tile, frame, pair = place // 4, place // 2 % 2, place % 2
        first = tile_block[place] * (2 * WT)
        for j in range(2):
            values = tok[pl.ds(pl.multiple_of(first + j * WT, WT), WT), :]
            for dy in range(2):
                row = 1 + tile * RL + (pair * 2 + j) * 2 + dy
                for dx in range(2):
                    lanes = (dy * 2 + dx) * LC
                    vol[frame, row, pl.ds(8 + dx, WT, stride=2), :] = values[:, lanes : lanes + LC]

    for frame in range(FT):
        spans = []
        for row in range(rows + 2):
            spans.append(
                jnp.concatenate(
                    [vol[frame, row, 7 + c : 7 + c + COLS, :] for c in range(3)], axis=-1
                ).astype(bf16)
            )
        for row in range(rows):
            patch[frame + 2, row] = jnp.concatenate(spans[row : row + 3], axis=-1)

    lane = lax.broadcasted_iota(jnp.int32, (8, RL * COLS), 1)
    line = lax.broadcasted_iota(jnp.int32, (8, RL * COLS), 0)
    in_band = (lane % COLS) // (COLS // 4) == line % 4
    high_line = line < 4
    pooled = jnp.zeros((8, CO), f32)
    out_copy = pltpu.make_async_copy(dec, dec_hbm, sem)
    for turn in range(2):
        tile = me if turn == 0 else 1 - me
        tile_rows = pl.ds(pl.multiple_of(tile * RL, RL), RL)
        for frame in range(FT):
            pre = bias[...]
            for a in range(3):
                pre = pre + jnp.dot(
                    patch[frame + a, tile_rows].reshape(RL * COLS, 3 * width),
                    weight[a * 3 * width : (a + 1) * 3 * width, :],
                    preferred_element_type=f32,
                )
            if turn == 0:
                dec[0, frame] = pre.astype(bf16).reshape(RL, COLS, CO)
            act = (0.5 * pre) * (1.0 + jnp.tanh(0.5 * pre))
            own = jnp.concatenate(
                [pool[tile, frame * RL + i : frame * RL + i + 1, :] for i in range(RL)], axis=-1
            )
            high = own.astype(bf16).astype(f32)
            terms = jnp.where(in_band, jnp.where(high_line, high, own - high), 0.0)
            pooled = pooled + jnp.dot(
                terms.astype(bf16), act.astype(bf16), preferred_element_type=f32
            )
        if turn == 0:
            out_copy.start()
    total = (pooled[:4] + pooled[4:]) * (1.0 / math.sqrt(2 * FT * RL * COLS // 4))
    for i in range(BPD):
        line_out = jnp.zeros((1, CO), f32)
        for band in range(4):
            line_out = jnp.where(owner_slot[band] == me * BPD + i, total[band : band + 1], line_out)
        policy[i : i + 1, :] = line_out
    out_copy.wait()


def decode(lat, conv_weight, conv_bias, pool, tile_block, owner_slot):
    vmem = pl.BlockSpec(memory_space=pltpu.VMEM)
    smem = pl.BlockSpec(memory_space=pltpu.SMEM)
    bf16, f32 = jnp.bfloat16, jnp.float32
    dec_shape = (1, FT, RL, COLS, CO)
    return pl.pallas_call(
        decode_kernel,
        out_shape=[jax.ShapeDtypeStruct(dec_shape, bf16), jax.ShapeDtypeStruct((BPD, CO), f32)],
        in_specs=[vmem] * 4 + [smem] * 2,
        out_specs=[pl.BlockSpec(memory_space=pl.ANY), vmem],
        scratch_shapes=[
            pltpu.VMEM((2 * S_DEV, 4 * LC), f32),
            pltpu.VMEM((FT, 2 * RL + 2, COLS + 16, LC), f32),
            pltpu.VMEM((FT + 2, 2 * RL, COLS, 9 * LC), bf16),
            pltpu.VMEM(dec_shape, bf16),
            pltpu.SemaphoreType.DMA,
        ],
        compiler_params=pltpu.CompilerParams(vmem_limit_bytes=60 * 2**20),
    )(lat, conv_weight, conv_bias.reshape(1, CO), pool, tile_block, owner_slot)


def local_pair(
    queries,
    keys_in,
    values_in,
    latent_proj,
    conv_weight,
    conv_bias,
    pool_weight,
    tile_block,
    owner_slot,
):
    lat, pool = attend(queries, keys_in, values_in, latent_proj, pool_weight)
    decoded, policy = decode(lat, conv_weight, conv_bias, pool, tile_block, owner_slot)
    return (decoded, policy)


def solution(mesh):
    placed = (
        P(("roll", "seq"), None),
        P(("roll", "seq"), None),
        P(("roll", "seq"), None),
        P(),
        P(),
        P(),
        P("seq", None, None, None),
        P("roll"),
        P("roll"),
    )
    return jax.shard_map(
        local_pair if mesh.shape["seq"] == 2 else local_any,
        mesh=mesh,
        in_specs=placed,
        out_specs=(P(("roll", "seq"), None, None, None, None), P(("roll", "seq"), None)),
        check_vma=False,
    )
```

```python
import math

import jax
import jax.numpy as jnp
from jax import lax
from jax.experimental import pallas as pl
from jax.experimental.pallas import tpu as pltpu
from jax.sharding import PartitionSpec as P

H = 24
HD = 128
LC = 16
CO = 512
S_DEV = 256
RT = 4
WT = 32
TR = 2
BPD = 2
FT = 2
RL = 8
COLS = 64


def shifted(array, axis, by):
    length = lax.axis_size(axis)
    pairs = [(i, i + by) for i in range(length) if 0 <= i + by < length]
    return lax.ppermute(array, axis, pairs)


def swapped(array, axis, bit):
    return lax.ppermute(array, axis, [(i, i ^ 1 << bit) for i in range(lax.axis_size(axis))])


def heads_attention(query_all, key_all, value_all):
    length = query_all.shape[0]
    block_rows = min(512, length)
    score_scale = 1.0 / math.sqrt(query_all.shape[2])
    query_blocks = query_all.reshape(
        length // block_rows, block_rows, query_all.shape[1], query_all.shape[2]
    )

    def one_block(query_part):
        scores = (
            jnp.einsum("qhd,khd->hqk", query_part, key_all, preferred_element_type=jnp.float32)
            * score_scale
        )
        expo = jnp.exp(scores - jnp.max(scores, axis=-1, keepdims=True))
        totals = jnp.sum(expo, axis=-1, keepdims=True)
        mixed = jnp.einsum(
            "hqk,khd->qhd", expo.astype(jnp.bfloat16), value_all, preferred_element_type=jnp.float32
        )
        return (mixed / jnp.transpose(totals, (1, 0, 2))).astype(jnp.bfloat16)

    return lax.map(one_block, query_blocks).reshape(length, query_all.shape[1], query_all.shape[2])


def window_columns(volume):
    frame_count = volume.shape[0] - 2
    row_count = volume.shape[1] - 2
    col_count = volume.shape[2] - 2
    pieces = [
        volume[a : a + frame_count, b : b + row_count, c : c + col_count]
        for a in range(3)
        for b in range(3)
        for c in range(3)
    ]
    return jnp.concatenate(pieces, axis=-1).reshape(
        frame_count * row_count * col_count, 27 * volume.shape[3]
    )


def picked(blocks, order):
    count = blocks.shape[0]
    choose = (order[:, None] == jnp.arange(count, dtype=jnp.int32)[None, :]).astype(jnp.bfloat16)
    flat = jnp.dot(choose, blocks.reshape(count, -1), preferred_element_type=jnp.float32)
    return flat.astype(jnp.bfloat16).reshape(blocks.shape)


def local_any(
    queries,
    keys_in,
    values_in,
    latent_proj,
    conv_weight,
    conv_bias,
    pool_weight,
    tile_block,
    owner_slot,
):
    group_count = lax.axis_size("seq")
    my_index = lax.axis_index("seq")
    seq_len = S_DEV * group_count
    heads_dev = H // group_count
    quarter = S_DEV // 4

    def to_groups(matrix):
        return matrix.reshape(S_DEV, group_count, heads_dev, HD)

    query_all = lax.all_to_all(to_groups(queries), "seq", split_axis=1, concat_axis=0, tiled=True)
    key_all = lax.all_to_all(to_groups(keys_in), "seq", split_axis=1, concat_axis=0, tiled=True)
    value_all = lax.all_to_all(to_groups(values_in), "seq", split_axis=1, concat_axis=0, tiled=True)
    mixed = heads_attention(query_all[:, 0], key_all[:, 0], value_all[:, 0])[:, None]
    flat_heads = mixed.reshape(seq_len, heads_dev * HD)
    ordered = picked(flat_heads.reshape(4 * group_count, quarter, heads_dev * HD), tile_block)
    ordered = ordered.reshape(seq_len, 1, heads_dev, HD)
    returned = lax.all_to_all(ordered, "seq", split_axis=0, concat_axis=1, tiled=True)
    tile_heads = returned.reshape(S_DEV, H * HD)
    latent = jnp.dot(tile_heads, latent_proj, preferred_element_type=jnp.float32).astype(
        jnp.bfloat16
    )
    tile_latent = (
        latent.reshape(FT, RT, WT, 2, 2, LC).transpose(0, 1, 3, 2, 4, 5).reshape(FT, RL, COLS * LC)
    )
    earlier = shifted(tile_latent, "seq", TR)
    extended = jnp.concatenate([earlier, tile_latent], axis=0)
    band_row = my_index % TR
    upper_band = band_row == 0
    outgoing = jnp.where(upper_band, extended[:, RL - 1 :], extended[:, :1])
    incoming = swapped(outgoing, "seq", 0)
    above = jnp.where(upper_band, jnp.zeros_like(incoming), incoming)
    below = jnp.where(upper_band, incoming, jnp.zeros_like(incoming))
    volume = jnp.concatenate([above, extended, below], axis=1).reshape(FT + 2, RL + 2, COLS, LC)
    volume = jnp.pad(volume, ((0, 0), (0, 0), (1, 1), (0, 0)))
    pre_act = (
        jnp.dot(window_columns(volume), conv_weight, preferred_element_type=jnp.float32) + conv_bias
    )
    decoded = pre_act.astype(jnp.bfloat16).reshape(1, FT, RL, COLS, CO)
    block_count = BPD * group_count
    band_voxels = group_count // TR * FT * TR * RL * (COLS // block_count)
    weighted = jax.nn.silu(pre_act).reshape(FT, RL, COLS, CO) * pool_weight[0][..., None]
    pooled_term = jnp.sum(weighted, axis=(0, 1)).reshape(block_count, COLS // block_count, CO).sum(
        axis=1
    ) / math.sqrt(band_voxels)
    total_pooled = lax.psum(pooled_term.astype(jnp.bfloat16), "seq").astype(jnp.float32)
    wanted_rows = my_index * BPD + jnp.arange(BPD, dtype=jnp.int32)
    chooser = (owner_slot[None, :] == wanted_rows[:, None]).astype(jnp.float32)
    policy = jnp.dot(
        chooser, total_pooled, precision=lax.Precision.HIGHEST, preferred_element_type=jnp.float32
    )
    return (decoded, policy)


SCALE2 = math.log2(math.e) / math.sqrt(HD)
HALF = S_DEV // 2
COLG = 3
GH = H // COLG
GW = GH * HD
NT = (((1,), (1,)), ((), ()))


def attend_kernel(
    q_hbm,
    k_hbm,
    v_hbm,
    w_hbm,
    pool,
    lat_out,
    pool_out,
    q,
    k,
    v,
    w,
    q_in,
    v_t,
    w_t,
    own,
    top_own,
    stat_own,
    stat_in,
    ret,
    ret_in,
    ret_level,
    level_in,
    lat_own,
    lat_in,
    pool_in,
    load_sem,
    q_send,
    q_recv,
    small_send,
    small_recv,
):
    me = lax.axis_index("seq")
    other = 1 - me
    loads = [
        pltpu.make_async_copy(src, dst, load_sem.at[i])
        for i, (src, dst) in enumerate(((q_hbm, q), (k_hbm, k), (v_hbm, v), (w_hbm, w)))
    ]
    for load in loads:
        load.start()

    barrier = pltpu.get_barrier_semaphore()
    pl.semaphore_signal(barrier, inc=1, device_id={"seq": other})
    pl.semaphore_wait(barrier, 1)

    def query_copy(half, group, piece):
        rows = pl.ds(half * HALF, HALF)
        start = group * GW + piece * (GW // 2)
        if not isinstance(group, int):
            start = pl.multiple_of(start, GW // 2)
        slot = (half * COLG + group) * 2 + piece
        part = (rows, pl.ds(start, GW // 2))
        return pltpu.make_async_remote_copy(
            src_ref=q_hbm.at[part],
            dst_ref=q_in.at[part],
            send_sem=q_send.at[slot],
            recv_sem=q_recv.at[slot],
            device_id={"seq": other},
        )

    def small_copy(src, dst, slot):
        return pltpu.make_async_remote_copy(
            src_ref=src,
            dst_ref=dst,
            send_sem=small_send.at[slot],
            recv_sem=small_recv.at[slot],
            device_id={"seq": other},
        )

    for group in range(COLG):
        query_copy(0, group, 0).start()
        query_copy(0, group, 1).start()
    for load in loads:
        load.wait()

    def head_cols(head):
        return pl.ds(pl.multiple_of(head * HD, HD), HD)

    def softmax(scores):
        top = jnp.max(scores, axis=0, keepdims=True)
        expo = jnp.exp2((scores - top) * SCALE2)
        top = top * SCALE2
        level = top + jnp.log(jnp.sum(expo, axis=0, keepdims=True)) * math.log2(math.e)
        return expo.astype(jnp.bfloat16), top, level

    def own_group(group, _):
        tops, levels = [], []
        for j in range(GH):
            head = group * GH + j
            cols = head_cols(head)
            value_t = v[:, cols].T
            v_t[head] = value_t
            w_t[head] = w[:, cols]
            scores = lax.dot_general(k[:, cols], q[:, cols], NT, preferred_element_type=jnp.float32)
            probs, top, level = softmax(scores)
            own[head] = jnp.dot(value_t, probs, preferred_element_type=jnp.float32)
            tops.append(top)
            levels.append(level)
        heads = pl.ds(pl.multiple_of(group * GH, GH), GH)
        top_own[heads, :] = jnp.concatenate(tops, axis=0)
        stat_own[heads, :] = jnp.concatenate(levels, axis=0)
        return 0

    lax.fori_loop(0, COLG, own_group, 0)
    stat_copy = small_copy(stat_own, stat_in, 0)
    stat_copy.start()
    pool_copy = small_copy(pool, pool_in, 5)
    pool_copy.start()
    pool_out[me] = pool[...]
    for group in range(COLG):
        query_copy(1, group, 0).start()
        query_copy(1, group, 1).start()
    stat_copy.wait_recv()

    def share(top, level, level_b):
        most = jnp.maximum(level, level_b)
        both = jnp.exp2(level - most) + jnp.exp2(level_b - most)
        return jnp.exp2(top - most) / both

    def partner_group(half, group, acc):
        rows = pl.ds(half * HALF, HALF)
        first = group * GH if isinstance(group, int) else pl.multiple_of(group * GH, GH)
        heads = pl.ds(first, GH)
        levels_b = stat_in[heads, rows]
        levels = []
        for j in range(GH):
            if j % (GH // 2) == 0:
                query_copy(half, group, j // (GH // 2)).wait_recv()
            head = group * GH + j
            cols = head_cols(head)
            scores = lax.dot_general(
                k[:, cols], q_in[rows, cols], NT, preferred_element_type=jnp.float32
            )
            probs, top, level = softmax(scores)
            mixed = jnp.dot(v_t[head], probs, preferred_element_type=jnp.float32)
            part = share(top, level, levels_b[j : j + 1])
            acc = acc + jnp.dot(
                w_t[head], (mixed * part).astype(jnp.bfloat16), preferred_element_type=jnp.float32
            )
            levels.append(level)
        ret_level[half, heads, :] = jnp.concatenate(levels, axis=0)
        return acc

    ret_copies = [small_copy(ret.at[half], ret_in.at[half], 1 + half) for half in range(2)]
    level_copies = [
        small_copy(ret_level.at[half], level_in.at[half], 6 + half) for half in range(2)
    ]
    lat_copies = [small_copy(lat_own.at[half], lat_in.at[half], 3 + half) for half in range(2)]

    def send_ret(half, acc):
        level_copies[half].start()
        ret[half] = acc.astype(jnp.bfloat16)
        ret_copies[half].start()

    def finish(half):
        rows = pl.ds(half * HALF, HALF)
        level_copies[half].wait_recv()
        part = share(top_own[:, rows], stat_own[:, rows], level_in[half])
        ret_copies[half].wait_recv()
        acc = ret_in[half].astype(jnp.float32)
        for head in range(H):
            acc = acc + jnp.dot(
                w_t[head],
                (own[head, :, rows] * part[head : head + 1]).astype(jnp.bfloat16),
                preferred_element_type=jnp.float32,
            )
        lat_own[half] = acc.astype(jnp.bfloat16)
        lat_copies[half].start()
        lat_out[me, half] = lat_own[half]

    zero = jnp.zeros((4 * LC, HALF), jnp.float32)
    acc = lax.fori_loop(0, COLG, lambda g, a: partner_group(0, g, a), zero)
    send_ret(0, acc)
    acc = partner_group(1, 0, zero)
    finish(0)
    acc = lax.fori_loop(1, COLG, lambda g, a: partner_group(1, g, a), acc)
    send_ret(1, acc)
    finish(1)
    pool_copy.wait_recv()
    pool_out[other] = pool_in[...]
    for half in range(2):
        lat_copies[half].wait_recv()
        lat_out[other, half] = lat_in[half]
    for half in range(2):
        for group in range(COLG):
            query_copy(half, group, 0).wait_send()
            query_copy(half, group, 1).wait_send()
    for copy in [stat_copy, pool_copy, *level_copies, *ret_copies, *lat_copies]:
        copy.wait_send()


def attend(queries, keys_in, values_in, latent_proj, pool_weight):
    width = H * HD
    any_spec = pl.BlockSpec(memory_space=pl.ANY)
    bf16, f32 = jnp.bfloat16, jnp.float32
    return pl.pallas_call(
        attend_kernel,
        out_shape=[
            jax.ShapeDtypeStruct((2, 2, 4 * LC, HALF), bf16),
            jax.ShapeDtypeStruct((2, FT * RL, COLS), f32),
        ],
        in_specs=[any_spec] * 4 + [pl.BlockSpec(memory_space=pltpu.VMEM)],
        out_specs=[pl.BlockSpec(memory_space=pltpu.VMEM)] * 2,
        scratch_shapes=[
            pltpu.VMEM((S_DEV, width), bf16),
            pltpu.VMEM((S_DEV, width), bf16),
            pltpu.VMEM((S_DEV, width), bf16),
            pltpu.VMEM((4 * LC, width), bf16),
            pltpu.VMEM((S_DEV, width), bf16),
            pltpu.VMEM((H, HD, S_DEV), bf16),
            pltpu.VMEM((H, 4 * LC, HD), bf16),
            pltpu.VMEM((H, HD, S_DEV), f32),
            pltpu.VMEM((H, S_DEV), f32),
            pltpu.VMEM((H, S_DEV), f32),
            pltpu.VMEM((H, S_DEV), f32),
            pltpu.VMEM((2, 4 * LC, HALF), bf16),
            pltpu.VMEM((2, 4 * LC, HALF), bf16),
            pltpu.VMEM((2, H, HALF), f32),
            pltpu.VMEM((2, H, HALF), f32),
            pltpu.VMEM((2, 4 * LC, HALF), bf16),
            pltpu.VMEM((2, 4 * LC, HALF), bf16),
            pltpu.VMEM((FT * RL, COLS), f32),
            pltpu.SemaphoreType.DMA((4,)),
            pltpu.SemaphoreType.DMA((4 * COLG,)),
            pltpu.SemaphoreType.DMA((4 * COLG,)),
            pltpu.SemaphoreType.DMA((8,)),
            pltpu.SemaphoreType.DMA((8,)),
        ],
        compiler_params=pltpu.CompilerParams(
            collective_id=0, has_side_effects=True, vmem_limit_bytes=56 * 2**20
        ),
    )(queries, keys_in, values_in, latent_proj.T, pool_weight.reshape(FT * RL, COLS))


def decode_kernel(
    lat, weight, bias, pool, tile_block, owner_slot, dec_hbm, policy, tok, vol, patch, dec, sem
):
    me = lax.axis_index("seq")
    f32, bf16 = jnp.float32, jnp.bfloat16
    for part in range(2):
        for half in range(2):
            first = (part * 2 + half) * HALF
            tok[first : first + HALF, :] = lat[part, half].astype(f32).T

    rows, width = 2 * RL, 3 * LC
    vol[:, :1] = jnp.zeros((FT, 1, COLS + 16, LC), f32)
    vol[:, rows + 1 :] = jnp.zeros((FT, 1, COLS + 16, LC), f32)
    vol[:, :, :8] = jnp.zeros((FT, rows + 2, 8, LC), f32)
    vol[:, :, COLS + 8 :] = jnp.zeros((FT, rows + 2, 8, LC), f32)
    patch[:2] = jnp.zeros((2, rows, COLS, 3 * width), bf16)
    for place in range(8):
        tile, frame, pair = place // 4, place // 2 % 2, place % 2
        first = tile_block[place] * (2 * WT)
        for j in range(2):
            values = tok[pl.ds(pl.multiple_of(first + j * WT, WT), WT), :]
            for dy in range(2):
                row = 1 + tile * RL + (pair * 2 + j) * 2 + dy
                for dx in range(2):
                    lanes = (dy * 2 + dx) * LC
                    vol[frame, row, pl.ds(8 + dx, WT, stride=2), :] = values[:, lanes : lanes + LC]

    for frame in range(FT):
        spans = []
        for row in range(rows + 2):
            spans.append(
                jnp.concatenate(
                    [vol[frame, row, 7 + c : 7 + c + COLS, :] for c in range(3)], axis=-1
                ).astype(bf16)
            )
        for row in range(rows):
            patch[frame + 2, row] = jnp.concatenate(spans[row : row + 3], axis=-1)

    lane = lax.broadcasted_iota(jnp.int32, (8, RL * COLS), 1)
    line = lax.broadcasted_iota(jnp.int32, (8, RL * COLS), 0)
    in_band = (lane % COLS) // (COLS // 4) == line % 4
    high_line = line < 4
    pooled = jnp.zeros((8, CO), f32)
    out_copy = pltpu.make_async_copy(dec, dec_hbm, sem)
    for turn in range(2):
        tile = me if turn == 0 else 1 - me
        tile_rows = pl.ds(pl.multiple_of(tile * RL, RL), RL)
        for frame in range(FT):
            pre = bias[...]
            for a in range(3):
                pre = pre + jnp.dot(
                    patch[frame + a, tile_rows].reshape(RL * COLS, 3 * width),
                    weight[a * 3 * width : (a + 1) * 3 * width, :],
                    preferred_element_type=f32,
                )
            if turn == 0:
                dec[0, frame] = pre.astype(bf16).reshape(RL, COLS, CO)
            act = (0.5 * pre) * (1.0 + jnp.tanh(0.5 * pre))
            own = jnp.concatenate(
                [pool[tile, frame * RL + i : frame * RL + i + 1, :] for i in range(RL)], axis=-1
            )
            high = own.astype(bf16).astype(f32)
            terms = jnp.where(in_band, jnp.where(high_line, high, own - high), 0.0)
            pooled = pooled + jnp.dot(
                terms.astype(bf16), act.astype(bf16), preferred_element_type=f32
            )
        if turn == 0:
            out_copy.start()
    total = (pooled[:4] + pooled[4:]) * (1.0 / math.sqrt(2 * FT * RL * COLS // 4))
    for i in range(BPD):
        line_out = jnp.zeros((1, CO), f32)
        for band in range(4):
            line_out = jnp.where(owner_slot[band] == me * BPD + i, total[band : band + 1], line_out)
        policy[i : i + 1, :] = line_out
    out_copy.wait()


def decode(lat, conv_weight, conv_bias, pool, tile_block, owner_slot):
    vmem = pl.BlockSpec(memory_space=pltpu.VMEM)
    smem = pl.BlockSpec(memory_space=pltpu.SMEM)
    bf16, f32 = jnp.bfloat16, jnp.float32
    dec_shape = (1, FT, RL, COLS, CO)
    return pl.pallas_call(
        decode_kernel,
        out_shape=[jax.ShapeDtypeStruct(dec_shape, bf16), jax.ShapeDtypeStruct((BPD, CO), f32)],
        in_specs=[vmem] * 4 + [smem] * 2,
        out_specs=[pl.BlockSpec(memory_space=pl.ANY), vmem],
        scratch_shapes=[
            pltpu.VMEM((2 * S_DEV, 4 * LC), f32),
            pltpu.VMEM((FT, 2 * RL + 2, COLS + 16, LC), f32),
            pltpu.VMEM((FT + 2, 2 * RL, COLS, 9 * LC), bf16),
            pltpu.VMEM(dec_shape, bf16),
            pltpu.SemaphoreType.DMA,
        ],
        compiler_params=pltpu.CompilerParams(vmem_limit_bytes=60 * 2**20),
    )(lat, conv_weight, conv_bias.reshape(1, CO), pool, tile_block, owner_slot)


def local_pair(
    queries,
    keys_in,
    values_in,
    latent_proj,
    conv_weight,
    conv_bias,
    pool_weight,
    tile_block,
    owner_slot,
):
    lat, pool = attend(queries, keys_in, values_in, latent_proj, pool_weight)
    decoded, policy = decode(lat, conv_weight, conv_bias, pool, tile_block, owner_slot)
    return (decoded, policy)


def solution(mesh):
    placed = (
        P(("roll", "seq"), None),
        P(("roll", "seq"), None),
        P(("roll", "seq"), None),
        P(),
        P(),
        P(),
        P("seq", None, None, None),
        P("roll"),
        P("roll"),
    )
    return jax.shard_map(
        local_pair if mesh.shape["seq"] == 2 else local_any,
        mesh=mesh,
        in_specs=placed,
        out_specs=(P(("roll", "seq"), None, None, None, None), P(("roll", "seq"), None)),
        check_vma=False,
    )
```
